32 devices in a mesh: occ: 4 (over x, core), vir: 8 (over z, y).
Axes of the slice: x: 2, y: 2, z: 4, core: 2. Of those that a mesh axis runs over, the one named last changes fastest.
Arguments:
- amplitudes: bfloat16 [4096, 256], P(('vir', 'occ')), may hold values from -6 to 6
- pair_irrep: int32 [32], P('vir'), may hold values from 0 to 7
- integrals: bfloat16 [8, 8, 128, 512], P('vir', None, None, 'occ'), may hold values from -0.375 to 0.375
- panel_blocks: int32 [8, 8], P('vir'), may hold values from 0 to 7, each once within a row
- panel_owner: int32 [2], replicated, may hold values from 0 to 7
Outputs:
- ladder: bfloat16 [4096, 512], P('vir', 'occ')
The draws below stay inside these ranges and needn't reach their ends.
Inputs may be any that keep to these rules, and one draw needn't show every extreme that they name: Each row of panel_blocks names every irrep once.
All inputs are finite; a program needn't handle non-finite values.
Results may differ from the reference program's by a relative error of at most 0.001.
Values may be sent and summed in bfloat16 or wider, within the bound.
A program may use at most 64 MiB of HBM per device.

```python
import jax
import jax.numpy as jnp
from jax import lax

IRREPS = 8
STEPS = 2
PAIR_DEV = 128
KB = 128
TILES = 32
PAIRS = 4096
COLS = 512
N_VIR = 8


def place_ends(values, own_key, low, largest):
    shape = values.shape
    place = [jax.random.randint(jax.random.fold_in(own_key, axis), (), 0, shape[axis]) for axis in range(len(shape))]
    values = values.at[tuple(place)].set(low)
    longest = shape.index(max(shape))
    place[longest] = (place[longest] + 1) % shape[longest]
    return values.at[tuple(place)].set(largest)


def steps_of(stream_key, shape, pieces, smallest, high):
    loudness, own = 1.0, jax.random.fold_in(stream_key, 6)
    for position, blocks in pieces:
        heights = jnp.exp(jax.random.uniform(jax.random.fold_in(own, position), (blocks,), jnp.float32, smallest / len(pieces), high / len(pieces)))
        loudness = loudness * jnp.repeat(heights, shape[position] // blocks).reshape([-1 if axis == position else 1 for axis in range(len(shape))])
    return loudness


def scatter_about(key, dims, deviation, reach, split=(), kind=jnp.bfloat16):
    array = deviation * jax.random.normal(key, dims, jnp.float32)
    if split:
        array = array * steps_of(key, dims, split, -0.22, 0.18)
    return jnp.clip(array, -reach, reach).astype(kind)


def setup_inputs(seed: int = 0) -> dict:
    streams_of = jax.random.split(jax.random.key(seed), 6)
    return {
        "amplitudes": scatter_about(streams_of[0], (PAIRS, STEPS * KB), 1.0, 6.0, ((0, 32),)),
        "pair_irrep": place_ends(jax.random.randint(streams_of[1], (TILES,), 0, IRREPS), jax.random.fold_in(streams_of[1], 1), 0, IRREPS - 1).astype(jnp.int32),
        "integrals": scatter_about(streams_of[2], (N_VIR, IRREPS, KB, COLS), (STEPS * KB) ** -0.5, 0.375, ((0, 8), (3, 4))),
        "panel_blocks": jax.vmap(lambda own: jax.random.permutation(own, IRREPS))(jax.random.split(streams_of[3], N_VIR)).reshape((N_VIR, IRREPS)).astype(jnp.int32),
        "panel_owner": jax.random.randint(streams_of[4], (STEPS,), 0, N_VIR).astype(jnp.int32),
    }


def reference(amplitudes, pair_irrep, integrals, panel_blocks, panel_owner):
    irrep_ids = jnp.arange(IRREPS, dtype=jnp.int32)
    ordered = []
    for step_index in range(STEPS):
        blocks = panel_blocks[panel_owner[step_index]]
        matches = blocks[None, :] == irrep_ids[:, None]
        slot_ids = jnp.sum(jnp.where(matches, irrep_ids[None, :], 0), axis=1).astype(jnp.int32)
        ordered.append(jnp.take(integrals[panel_owner[step_index]], slot_ids, axis=0))
    amp_tiles = amplitudes.reshape(TILES, PAIR_DEV, STEPS * KB)

    def tile_ladder(inputs):
        tile_rows, irrep = inputs
        weights = jnp.concatenate(
            [lax.dynamic_index_in_dim(one_panel, irrep, 0, keepdims=False) for one_panel in ordered], axis=0)
        return jnp.dot(tile_rows, weights, preferred_element_type=jnp.float32).astype(jnp.bfloat16)

    ladder = lax.map(tile_ladder, (amp_tiles, pair_irrep))
    return ladder.reshape(PAIRS, COLS)
```

```python
import functools

import jax
import jax.numpy as jnp
from jax import lax
from jax.experimental import pallas as pl
from jax.experimental.pallas import tpu as pltpu
from jax.sharding import PartitionSpec as P

MESH = pl.DeviceIdType.MESH
ROWS = 16


def guarded(always, condition, run):
    if always:
        run()
    else:
        pl.when(condition)(run)


def ladder_kernel(
    n_vir, n_occ, relays, by_tile,
    labels_ref, blocks_ref, owner_ref, amp_ref, panel_ref, out_ref,
    info, info_all, info_smem, stage, got, picked, weights, amp_all,
    info_send, info_recv, one_send, one_recv, two_send, two_recv, amp_send, amp_recv, local_sem,
):
    vir, occ = lax.axis_index("vir"), lax.axis_index("occ")
    irreps = panel_ref.shape[0]
    steps = owner_ref.shape[0]
    tiles = labels_ref.shape[0]
    piece = stage.shape[2]
    pair_dev = amp_ref.shape[0]
    full = relays == n_vir
    is_relay = vir < relays

    barrier = pltpu.get_barrier_semaphore()
    for d in range(1, n_vir):
        pl.semaphore_signal(barrier, inc=1, device_id={"vir": lax.rem(vir + d, n_vir)}, device_id_type=MESH)
    for d in range(1, n_occ):
        pl.semaphore_signal(barrier, inc=1, device_id={"occ": lax.rem(occ + d, n_occ)}, device_id_type=MESH)

    lanes = lax.broadcasted_iota(jnp.int32, info.shape, 1)
    row = jnp.zeros(info.shape, jnp.int32)
    for t in range(tiles):
        row = jnp.where(lanes == t, labels_ref[t], row)
    info[...] = row
    info_all[vir] = row
    for g in range(irreps):
        slot = jnp.int32(0)
        for b in range(irreps):
            slot = jnp.where(blocks_ref[0, b] == g, b, slot)
        block = panel_ref[slot]
        for w in range(relays):
            stage[w, g] = block[w * piece:(w + 1) * piece]

    pl.semaphore_wait(barrier, n_vir - 1 + n_occ - 1)

    def info_copy(d):
        return pltpu.make_async_remote_copy(
            src_ref=info, dst_ref=info_all.at[vir], send_sem=info_send.at[d], recv_sem=info_recv.at[d],
            device_id={"vir": lax.rem(vir + d, n_vir)}, device_id_type=MESH)

    def one_copy(d):
        to = lax.rem(vir + d, n_vir)
        return pltpu.make_async_remote_copy(
            src_ref=stage.at[to], dst_ref=got.at[vir], send_sem=one_send.at[d], recv_sem=one_recv.at[d],
            device_id={"vir": to}, device_id_type=MESH)

    def two_copy(d):
        return pltpu.make_async_remote_copy(
            src_ref=picked.at[d if by_tile else 0],
            dst_ref=weights.at[:, :, pl.ds(pl.multiple_of(vir * piece, piece), piece), :],
            send_sem=two_send.at[d], recv_sem=two_recv.at[d],
            device_id={"vir": lax.rem(vir + d, n_vir)}, device_id_type=MESH)

    def amp_copy(d):
        return pltpu.make_async_remote_copy(
            src_ref=amp_ref, dst_ref=amp_all.at[occ], send_sem=amp_send.at[d], recv_sem=amp_recv.at[d],
            device_id={"occ": lax.rem(occ + d, n_occ)}, device_id_type=MESH)

    def wait_one_from_stage(d):
        pltpu.make_async_remote_copy(
            src_ref=stage.at[0], dst_ref=got.at[vir], send_sem=one_send.at[d], recv_sem=one_recv.at[d],
            device_id={"vir": lax.rem(vir + d, n_vir)}, device_id_type=MESH).wait_recv()

    if by_tile:
        for d in range(1, n_vir):
            guarded(full, lax.rem(vir + d, n_vir) < relays, lambda d=d: info_copy(d).start())
    for d in range(1, n_vir):
        guarded(full, lax.rem(vir + d, n_vir) < relays, lambda d=d: one_copy(d).start())
    for d in range(1, n_occ):
        amp_copy(d).start()

    amp_all[occ] = amp_ref[...]

    def relay():
        got[vir] = stage[vir]
        if by_tile:
            for d in range(1, n_vir):
                info_copy(d).wait_recv()
            to_smem = pltpu.make_async_copy(info_all, info_smem, local_sem)
            to_smem.start()
            to_smem.wait()
        for d in range(1, n_vir):
            wait_one_from_stage(d)
        owners = [owner_ref[s] for s in range(steps)]
        for d in list(range(1, n_vir)) + [0]:
            to = lax.rem(vir + d, n_vir)
            if by_tile:
                for t in range(tiles):
                    irrep = info_smem[to, 0, t]
                    for s in range(steps):
                        picked[d, t, s] = got[owners[s], irrep]
            elif d == 1 or n_vir == 1:
                for g in range(irreps):
                    for s in range(steps):
                        picked[0, g, s] = got[owners[s], g]
            if d:
                two_copy(d).start()
        weights[:, :, pl.ds(pl.multiple_of(vir * piece, piece), piece), :] = picked[0]

    guarded(full, is_relay, relay)

    for d in range(1, n_occ):
        amp_copy(d).wait_recv()
    for d in range(1, n_vir):
        guarded(full, lax.rem(vir + n_vir - d, n_vir) < relays, lambda d=d: two_copy(d).wait_recv())

    def tile(t):
        chosen = weights[t if by_tile else labels_ref[t]]
        chosen = chosen.reshape(chosen.shape[0] * chosen.shape[1], chosen.shape[2])
        result = jnp.dot(amp_all[t], chosen, preferred_element_type=jnp.float32)
        out_ref[pl.ds(pl.multiple_of(t * pair_dev, pair_dev), pair_dev), :] = result.astype(out_ref.dtype)

    if tiles <= 8:
        for t in range(tiles):
            tile(t)
    else:
        pl.loop(0, tiles)(tile)

    for d in range(1, n_occ):
        amp_copy(d).wait_send()
    for d in range(1, n_vir):
        if by_tile:
            guarded(full, lax.rem(vir + d, n_vir) < relays, lambda d=d: info_copy(d).wait_send())
        guarded(full, lax.rem(vir + d, n_vir) < relays, lambda d=d: one_copy(d).wait_send())
        guarded(full, is_relay, lambda d=d: two_copy(d).wait_send())


def per_device(n_vir, n_occ, amplitudes, pair_irrep, integrals, panel_blocks, panel_owner):
    pair_dev, width = amplitudes.shape
    _, irreps, depth, columns = integrals.shape
    tiles = pair_irrep.shape[0]
    steps = panel_owner.shape[0]
    relays = min(n_vir, depth // ROWS)
    piece = depth // relays
    by_tile = tiles < irreps
    choices = min(tiles, irreps)
    lanes = -(-tiles // 128) * 128
    kind = amplitudes.dtype
    smem = pl.BlockSpec(memory_space=pltpu.SMEM)
    vmem = pl.BlockSpec(memory_space=pltpu.VMEM)
    dma = pltpu.SemaphoreType.DMA
    return pl.pallas_call(
        functools.partial(ladder_kernel, n_vir, n_occ, relays, by_tile),
        out_shape=jax.ShapeDtypeStruct((tiles * pair_dev, columns), kind),
        in_specs=[smem, smem, smem, vmem, vmem],
        out_specs=vmem,
        scratch_shapes=[
            pltpu.VMEM((1, lanes), jnp.int32),
            pltpu.VMEM((n_vir, 1, lanes), jnp.int32),
            pltpu.SMEM((n_vir, 1, lanes), jnp.int32),
            pltpu.VMEM((relays, irreps, piece, columns), kind),
            pltpu.VMEM((n_vir, irreps, piece, columns), kind),
            pltpu.VMEM((n_vir if by_tile else 1, choices, steps, piece, columns), kind),
            pltpu.VMEM((choices, steps, depth, columns), kind),
            pltpu.VMEM((tiles, pair_dev, width), kind),
            dma((n_vir,)), dma((n_vir,)), dma((n_vir,)), dma((n_vir,)),
            dma((n_vir,)), dma((n_vir,)), dma((n_occ,)), dma((n_occ,)), dma,
        ],
        compiler_params=pltpu.CompilerParams(
            collective_id=0, has_side_effects=True, vmem_limit_bytes=32 * 1024 * 1024),
    )(pair_irrep, panel_blocks, panel_owner, amplitudes, integrals[0])


def solution(mesh):
    return jax.shard_map(
        functools.partial(per_device, mesh.shape["vir"], mesh.shape["occ"]),
        mesh=mesh,
        in_specs=(
            P(("vir", "occ"), None),
            P("vir"),
            P("vir", None, None, "occ"),
            P("vir", None),
            P(),
        ),
        out_specs=P("vir", "occ"),
        check_vma=False,
    )
```

```python
import functools

import jax
import jax.numpy as jnp
from jax import lax
from jax.experimental import pallas as pl
from jax.experimental.pallas import tpu as pltpu
from jax.sharding import PartitionSpec as P

MESH = pl.DeviceIdType.MESH
ROWS = 16


def guarded(always, condition, run):
    if always:
        run()
    else:
        pl.when(condition)(run)


def ladder_kernel(
    n_vir, n_occ, relays, by_tile,
    labels_hbm, blocks_hbm, owner_hbm, amp_ref, panel_hbm, out_ref,
    labels_ref, blocks_ref, owner_ref, panel_ref,
    info, info_all, info_smem, stage, got, picked, weights, amp_all,
    info_send, info_recv, one_send, one_recv, two_send, two_recv, amp_send, amp_recv, local_sem, fetch_sem,
):
    vir, occ = lax.axis_index("vir"), lax.axis_index("occ")
    irreps = panel_ref.shape[0]
    steps = owner_ref.shape[0]
    tiles = labels_ref.shape[0]
    piece = stage.shape[2]
    pair_dev = amp_ref.shape[0]
    full = relays == n_vir
    is_relay = vir < relays

    barrier = pltpu.get_barrier_semaphore()
    for d in range(1, n_vir):
        pl.semaphore_signal(barrier, inc=1, device_id={"vir": lax.rem(vir + d, n_vir)}, device_id_type=MESH)
    for d in range(1, n_occ):
        pl.semaphore_signal(barrier, inc=1, device_id={"occ": lax.rem(occ + d, n_occ)}, device_id_type=MESH)

    fetches = [
        pltpu.make_async_copy(labels_hbm, labels_ref, fetch_sem.at[0]),
        pltpu.make_async_copy(blocks_hbm, blocks_ref, fetch_sem.at[1]),
        pltpu.make_async_copy(owner_hbm, owner_ref, fetch_sem.at[2]),
        pltpu.make_async_copy(panel_hbm.at[0], panel_ref, fetch_sem.at[3]),
        pltpu.make_async_copy(amp_ref, amp_all.at[occ], fetch_sem.at[4]),
    ]
    for fetch in fetches:
        fetch.start()
    for fetch in fetches:
        fetch.wait()

    lanes = lax.broadcasted_iota(jnp.int32, info.shape, 1)
    row = jnp.zeros(info.shape, jnp.int32)
    for t in range(tiles):
        row = jnp.where(lanes == t, labels_ref[t], row)
    info[...] = row
    info_all[vir] = row
    for g in range(irreps):
        slot = jnp.int32(0)
        for b in range(irreps):
            slot = jnp.where(blocks_ref[0, b] == g, b, slot)
        block = panel_ref[slot]
        for w in range(relays):
            stage[w, g] = block[w * piece:(w + 1) * piece]

    pl.semaphore_wait(barrier, n_vir - 1 + n_occ - 1)

    def info_copy(d):
        return pltpu.make_async_remote_copy(
            src_ref=info, dst_ref=info_all.at[vir], send_sem=info_send.at[d], recv_sem=info_recv.at[d],
            device_id={"vir": lax.rem(vir + d, n_vir)}, device_id_type=MESH)

    def one_copy(d):
        to = lax.rem(vir + d, n_vir)
        return pltpu.make_async_remote_copy(
            src_ref=stage.at[to], dst_ref=got.at[vir], send_sem=one_send.at[d], recv_sem=one_recv.at[d],
            device_id={"vir": to}, device_id_type=MESH)

    def two_copy(d):
        return pltpu.make_async_remote_copy(
            src_ref=picked.at[d if by_tile else 0],
            dst_ref=weights.at[:, :, pl.ds(pl.multiple_of(vir * piece, piece), piece), :],
            send_sem=two_send.at[d], recv_sem=two_recv.at[d],
            device_id={"vir": lax.rem(vir + d, n_vir)}, device_id_type=MESH)

    def amp_copy(d):
        return pltpu.make_async_remote_copy(
            src_ref=amp_ref, dst_ref=amp_all.at[occ], send_sem=amp_send.at[d], recv_sem=amp_recv.at[d],
            device_id={"occ": lax.rem(occ + d, n_occ)}, device_id_type=MESH)

    def wait_one_from_stage(d):
        pltpu.make_async_remote_copy(
            src_ref=stage.at[0], dst_ref=got.at[vir], send_sem=one_send.at[d], recv_sem=one_recv.at[d],
            device_id={"vir": lax.rem(vir + d, n_vir)}, device_id_type=MESH).wait_recv()

    if by_tile:
        for d in range(1, n_vir):
            guarded(full, lax.rem(vir + d, n_vir) < relays, lambda d=d: info_copy(d).start())
    for d in range(1, n_vir):
        guarded(full, lax.rem(vir + d, n_vir) < relays, lambda d=d: one_copy(d).start())
    for d in range(1, n_occ):
        amp_copy(d).start()

    def relay():
        got[vir] = stage[vir]
        if by_tile:
            for d in range(1, n_vir):
                info_copy(d).wait_recv()
            to_smem = pltpu.make_async_copy(info_all, info_smem, local_sem)
            to_smem.start()
            to_smem.wait()
        for d in range(1, n_vir):
            wait_one_from_stage(d)
        owners = [owner_ref[s] for s in range(steps)]
        for d in list(range(1, n_vir)) + [0]:
            to = lax.rem(vir + d, n_vir)
            if by_tile:
                for t in range(tiles):
                    irrep = info_smem[to, 0, t]
                    for s in range(steps):
                        picked[d, t, s] = got[owners[s], irrep]
            elif d == 1 or n_vir == 1:
                for g in range(irreps):
                    for s in range(steps):
                        picked[0, g, s] = got[owners[s], g]
            if d:
                two_copy(d).start()
        weights[:, :, pl.ds(pl.multiple_of(vir * piece, piece), piece), :] = picked[0]

    guarded(full, is_relay, relay)

    for d in range(1, n_occ):
        amp_copy(d).wait_recv()
    for d in range(1, n_vir):
        guarded(full, lax.rem(vir + n_vir - d, n_vir) < relays, lambda d=d: two_copy(d).wait_recv())

    def tile(t):
        chosen = weights[t if by_tile else labels_ref[t]]
        chosen = chosen.reshape(chosen.shape[0] * chosen.shape[1], chosen.shape[2])
        result = jnp.dot(amp_all[t], chosen, preferred_element_type=jnp.float32)
        out_ref[pl.ds(pl.multiple_of(t * pair_dev, pair_dev), pair_dev), :] = result.astype(out_ref.dtype)

    if tiles <= 8:
        for t in range(tiles):
            tile(t)
    else:
        pl.loop(0, tiles)(tile)

    for d in range(1, n_occ):
        amp_copy(d).wait_send()
    for d in range(1, n_vir):
        if by_tile:
            guarded(full, lax.rem(vir + d, n_vir) < relays, lambda d=d: info_copy(d).wait_send())
        guarded(full, lax.rem(vir + d, n_vir) < relays, lambda d=d: one_copy(d).wait_send())
        guarded(full, is_relay, lambda d=d: two_copy(d).wait_send())


def per_device(n_vir, n_occ, amplitudes, pair_irrep, integrals, panel_blocks, panel_owner):
    pair_dev, width = amplitudes.shape
    _, irreps, depth, columns = integrals.shape
    tiles = pair_irrep.shape[0]
    steps = panel_owner.shape[0]
    relays = min(n_vir, depth // ROWS)
    piece = depth // relays
    by_tile = tiles < irreps
    choices = min(tiles, irreps)
    lanes = -(-tiles // 128) * 128
    kind = amplitudes.dtype
    hbm = pl.BlockSpec(memory_space=pltpu.HBM)
    dma = pltpu.SemaphoreType.DMA
    return pl.pallas_call(
        functools.partial(ladder_kernel, n_vir, n_occ, relays, by_tile),
        out_shape=jax.ShapeDtypeStruct((tiles * pair_dev, columns), kind),
        in_specs=[hbm] * 5,
        out_specs=pl.BlockSpec(memory_space=pltpu.VMEM),
        scratch_shapes=[
            pltpu.SMEM(pair_irrep.shape, jnp.int32),
            pltpu.SMEM(panel_blocks.shape, jnp.int32),
            pltpu.SMEM(panel_owner.shape, jnp.int32),
            pltpu.VMEM(integrals.shape[1:], kind),
            pltpu.VMEM((1, lanes), jnp.int32),
            pltpu.VMEM((n_vir, 1, lanes), jnp.int32),
            pltpu.SMEM((n_vir, 1, lanes), jnp.int32),
            pltpu.VMEM((relays, irreps, piece, columns), kind),
            pltpu.VMEM((n_vir, irreps, piece, columns), kind),
            pltpu.VMEM((n_vir if by_tile else 1, choices, steps, piece, columns), kind),
            pltpu.VMEM((choices, steps, depth, columns), kind),
            pltpu.VMEM((tiles, pair_dev, width), kind),
            dma((n_vir,)), dma((n_vir,)), dma((n_vir,)), dma((n_vir,)),
            dma((n_vir,)), dma((n_vir,)), dma((n_occ,)), dma((n_occ,)), dma, dma((5,)),
        ],
        compiler_params=pltpu.CompilerParams(
            collective_id=0, has_side_effects=True, vmem_limit_bytes=60 * 1024 * 1024),
    )(pair_irrep, panel_blocks, panel_owner, amplitudes, integrals)


def solution(mesh):
    return jax.shard_map(
        functools.partial(per_device, mesh.shape["vir"], mesh.shape["occ"]),
        mesh=mesh,
        in_specs=(
            P(("vir", "occ"), None),
            P("vir"),
            P("vir", None, None, "occ"),
            P("vir", None),
            P(),
        ),
        out_specs=P("vir", "occ"),
        check_vma=False,
    )
```

```python
import functools

import jax
import jax.numpy as jnp
from jax import lax
from jax.experimental import pallas as pl
from jax.experimental.pallas import tpu as pltpu
from jax.sharding import PartitionSpec as P

MESH = pl.DeviceIdType.MESH
ROWS = 16


def guarded(always, condition, run):
    if always:
        run()
    else:
        pl.when(condition)(run)


def ladder_kernel(
    n_vir, n_occ, relays, by_tile,
    labels_hbm, blocks_hbm, owner_hbm, amp_ref, panel_hbm, amp_all, weights,
    labels_ref, blocks_ref, owner_ref, panel_ref,
    info, info_all, info_smem, stage, got, picked,
    info_send, info_recv, one_send, one_recv, two_send, two_recv, amp_send, amp_recv, local_sem, fetch_sem,
):
    vir, occ = lax.axis_index("vir"), lax.axis_index("occ")
    irreps = panel_ref.shape[0]
    steps = owner_ref.shape[0]
    tiles = labels_ref.shape[0]
    piece = stage.shape[2]
    full = relays == n_vir
    is_relay = vir < relays

    barrier = pltpu.get_barrier_semaphore()
    for d in range(1, n_vir):
        pl.semaphore_signal(barrier, inc=1, device_id={"vir": lax.rem(vir + d, n_vir)}, device_id_type=MESH)
    for d in range(1, n_occ):
        pl.semaphore_signal(barrier, inc=1, device_id={"occ": lax.rem(occ + d, n_occ)}, device_id_type=MESH)

    fetches = [
        pltpu.make_async_copy(labels_hbm, labels_ref, fetch_sem.at[0]),
        pltpu.make_async_copy(blocks_hbm, blocks_ref, fetch_sem.at[1]),
        pltpu.make_async_copy(owner_hbm, owner_ref, fetch_sem.at[2]),
        pltpu.make_async_copy(panel_hbm.at[0], panel_ref, fetch_sem.at[3]),
        pltpu.make_async_copy(amp_ref, amp_all.at[occ], fetch_sem.at[4]),
    ]
    for fetch in fetches:
        fetch.start()
    for fetch in fetches[:4]:
        fetch.wait()

    lanes = lax.broadcasted_iota(jnp.int32, info.shape, 1)
    row = jnp.zeros(info.shape, jnp.int32)
    for t in range(tiles):
        row = jnp.where(lanes == t, labels_ref[t], row)
    info[...] = row
    info_all[vir] = row
    for g in range(irreps):
        slot = jnp.int32(0)
        for b in range(irreps):
            slot = jnp.where(blocks_ref[0, b] == g, b, slot)
        block = panel_ref[slot]
        for w in range(relays):
            stage[w, g] = block[w * piece:(w + 1) * piece]

    pl.semaphore_wait(barrier, n_vir - 1 + n_occ - 1)

    def info_copy(d):
        return pltpu.make_async_remote_copy(
            src_ref=info, dst_ref=info_all.at[vir], send_sem=info_send.at[d], recv_sem=info_recv.at[d],
            device_id={"vir": lax.rem(vir + d, n_vir)}, device_id_type=MESH)

    def one_copy(d):
        to = lax.rem(vir + d, n_vir)
        return pltpu.make_async_remote_copy(
            src_ref=stage.at[to], dst_ref=got.at[vir], send_sem=one_send.at[d], recv_sem=one_recv.at[d],
            device_id={"vir": to}, device_id_type=MESH)

    def two_copy(d):
        return pltpu.make_async_remote_copy(
            src_ref=picked.at[d if by_tile else 0],
            dst_ref=weights.at[:, :, pl.ds(pl.multiple_of(vir * piece, piece), piece), :],
            send_sem=two_send.at[d], recv_sem=two_recv.at[d],
            device_id={"vir": lax.rem(vir + d, n_vir)}, device_id_type=MESH)

    def own_rows():
        return pltpu.make_async_copy(
            picked.at[0], weights.at[:, :, pl.ds(pl.multiple_of(vir * piece, piece), piece), :], local_sem)

    def amp_copy(d):
        return pltpu.make_async_remote_copy(
            src_ref=amp_ref, dst_ref=amp_all.at[occ], send_sem=amp_send.at[d], recv_sem=amp_recv.at[d],
            device_id={"occ": lax.rem(occ + d, n_occ)}, device_id_type=MESH)

    def wait_one_from_stage(d):
        pltpu.make_async_remote_copy(
            src_ref=stage.at[0], dst_ref=got.at[vir], send_sem=one_send.at[d], recv_sem=one_recv.at[d],
            device_id={"vir": lax.rem(vir + d, n_vir)}, device_id_type=MESH).wait_recv()

    if by_tile:
        for d in range(1, n_vir):
            guarded(full, lax.rem(vir + d, n_vir) < relays, lambda d=d: info_copy(d).start())
    for d in range(1, n_vir):
        guarded(full, lax.rem(vir + d, n_vir) < relays, lambda d=d: one_copy(d).start())
    for d in range(1, n_occ):
        amp_copy(d).start()

    def relay():
        got[vir] = stage[vir]
        if by_tile:
            for d in range(1, n_vir):
                info_copy(d).wait_recv()
            to_smem = pltpu.make_async_copy(info_all, info_smem, local_sem)
            to_smem.start()
            to_smem.wait()
        for d in range(1, n_vir):
            wait_one_from_stage(d)
        owners = [owner_ref[s] for s in range(steps)]
        for d in list(range(1, n_vir)) + [0]:
            to = lax.rem(vir + d, n_vir)
            if by_tile:
                for t in range(tiles):
                    irrep = info_smem[to, 0, t]
                    for s in range(steps):
                        picked[d, t, s] = got[owners[s], irrep]
            elif d == 1 or n_vir == 1:
                for g in range(irreps):
                    for s in range(steps):
                        picked[0, g, s] = got[owners[s], g]
            if d:
                two_copy(d).start()
        own_rows().start()

    guarded(full, is_relay, relay)

    for d in range(1, n_occ):
        amp_copy(d).wait_recv()
    for d in range(1, n_vir):
        guarded(full, lax.rem(vir + n_vir - d, n_vir) < relays, lambda d=d: two_copy(d).wait_recv())

    fetches[4].wait()
    guarded(full, is_relay, lambda: own_rows().wait())
    for d in range(1, n_occ):
        amp_copy(d).wait_send()
    for d in range(1, n_vir):
        if by_tile:
            guarded(full, lax.rem(vir + d, n_vir) < relays, lambda d=d: info_copy(d).wait_send())
        guarded(full, lax.rem(vir + d, n_vir) < relays, lambda d=d: one_copy(d).wait_send())
        guarded(full, is_relay, lambda d=d: two_copy(d).wait_send())


def per_device(n_vir, n_occ, amplitudes, pair_irrep, integrals, panel_blocks, panel_owner):
    pair_dev, width = amplitudes.shape
    _, irreps, depth, columns = integrals.shape
    tiles = pair_irrep.shape[0]
    steps = panel_owner.shape[0]
    relays = min(n_vir, depth // ROWS)
    piece = depth // relays
    by_tile = tiles < irreps
    choices = min(tiles, irreps)
    lanes = -(-tiles // 128) * 128
    kind = amplitudes.dtype
    hbm = pl.BlockSpec(memory_space=pltpu.HBM)
    dma = pltpu.SemaphoreType.DMA
    gathered, weights = pl.pallas_call(
        functools.partial(ladder_kernel, n_vir, n_occ, relays, by_tile),
        out_shape=(
            jax.ShapeDtypeStruct((tiles, pair_dev, width), kind),
            jax.ShapeDtypeStruct((choices, steps, depth, columns), kind),
        ),
        in_specs=[hbm] * 5,
        out_specs=(hbm, hbm),
        scratch_shapes=[
            pltpu.SMEM(pair_irrep.shape, jnp.int32),
            pltpu.SMEM(panel_blocks.shape, jnp.int32),
            pltpu.SMEM(panel_owner.shape, jnp.int32),
            pltpu.VMEM(integrals.shape[1:], kind),
            pltpu.VMEM((1, lanes), jnp.int32),
            pltpu.VMEM((n_vir, 1, lanes), jnp.int32),
            pltpu.SMEM((n_vir, 1, lanes), jnp.int32),
            pltpu.VMEM((relays, irreps, piece, columns), kind),
            pltpu.VMEM((n_vir, irreps, piece, columns), kind),
            pltpu.VMEM((n_vir if by_tile else 1, choices, steps, piece, columns), kind),
            dma((n_vir,)), dma((n_vir,)), dma((n_vir,)), dma((n_vir,)),
            dma((n_vir,)), dma((n_vir,)), dma((n_occ,)), dma((n_occ,)), dma, dma((5,)),
        ],
        compiler_params=pltpu.CompilerParams(
            collective_id=0, has_side_effects=True, vmem_limit_bytes=60 * 1024 * 1024),
    )(pair_irrep, panel_blocks, panel_owner, amplitudes, integrals)
    weights = weights.reshape(choices, steps * depth, columns)
    if by_tile:
        result = jnp.einsum("tpk,tkc->tpc", gathered, weights, preferred_element_type=jnp.float32)
        return result.astype(kind).reshape(tiles * pair_dev, columns)

    def tile_ladder(inputs):
        rows, irrep = inputs
        chosen = lax.dynamic_index_in_dim(weights, irrep, 0, keepdims=False)
        return jnp.dot(rows, chosen, preferred_element_type=jnp.float32).astype(kind)

    return lax.map(tile_ladder, (gathered, pair_irrep)).reshape(tiles * pair_dev, columns)


def solution(mesh):
    return jax.shard_map(
        functools.partial(per_device, mesh.shape["vir"], mesh.shape["occ"]),
        mesh=mesh,
        in_specs=(
            P(("vir", "occ"), None),
            P("vir"),
            P("vir", None, None, "occ"),
            P("vir", None),
            P(),
        ),
        out_specs=P("vir", "occ"),
        check_vma=False,
    )
```

```python
import functools

import jax
import jax.numpy as jnp
from jax import lax
from jax.experimental import pallas as pl
from jax.experimental.pallas import tpu as pltpu
from jax.sharding import PartitionSpec as P

MESH = pl.DeviceIdType.MESH
ROWS = 16


def guarded(always, condition, run):
    if always:
        run()
    else:
        pl.when(condition)(run)


def ladder_kernel(
    n_vir, n_occ, relays, by_tile,
    labels_hbm, blocks_hbm, owner_hbm, amp_ref, panel_hbm, amp_all, weights,
    labels_ref, blocks_ref, owner_ref, panel_ref,
    info, info_all, info_smem, stage, got, picked,
    info_send, info_recv, one_send, one_recv, two_send, two_recv, amp_send, amp_recv, local_sem, fetch_sem,
):
    vir, occ = lax.axis_index("vir"), lax.axis_index("occ")
    irreps = panel_ref.shape[0]
    steps = owner_ref.shape[0]
    tiles = labels_ref.shape[0]
    piece = stage.shape[2]
    full = relays == n_vir
    is_relay = vir < relays

    barrier = pltpu.get_barrier_semaphore()
    for d in range(1, n_vir):
        pl.semaphore_signal(barrier, inc=1, device_id={"vir": lax.rem(vir + d, n_vir)}, device_id_type=MESH)
    for d in range(1, n_occ):
        pl.semaphore_signal(barrier, inc=1, device_id={"occ": lax.rem(occ + d, n_occ)}, device_id_type=MESH)

    fetches = [
        pltpu.make_async_copy(labels_hbm, labels_ref, fetch_sem.at[0]),
        pltpu.make_async_copy(blocks_hbm, blocks_ref, fetch_sem.at[1]),
        pltpu.make_async_copy(owner_hbm, owner_ref, fetch_sem.at[2]),
        pltpu.make_async_copy(panel_hbm.at[0], panel_ref, fetch_sem.at[3]),
        pltpu.make_async_copy(amp_ref, amp_all.at[occ], fetch_sem.at[4]),
    ]
    for fetch in fetches:
        fetch.start()
    for fetch in fetches[:4]:
        fetch.wait()

    lanes = lax.broadcasted_iota(jnp.int32, info.shape, 1)
    row = jnp.zeros(info.shape, jnp.int32)
    for t in range(tiles):
        row = jnp.where(lanes == t, labels_ref[t], row)
    info[...] = row
    info_all[vir] = row
    for g in range(irreps):
        slot = jnp.int32(0)
        for b in range(irreps):
            slot = jnp.where(blocks_ref[0, b] == g, b, slot)
        block = panel_ref[slot]
        for w in range(relays):
            stage[w, g] = block[w * piece:(w + 1) * piece]

    pl.semaphore_wait(barrier, n_vir - 1 + n_occ - 1)

    def info_copy(d):
        return pltpu.make_async_remote_copy(
            src_ref=info, dst_ref=info_all.at[vir], send_sem=info_send.at[d], recv_sem=info_recv.at[d],
            device_id={"vir": lax.rem(vir + d, n_vir)}, device_id_type=MESH)

    def one_copy(d):
        to = lax.rem(vir + d, n_vir)
        return pltpu.make_async_remote_copy(
            src_ref=stage.at[to], dst_ref=got.at[vir], send_sem=one_send.at[d], recv_sem=one_recv.at[d],
            device_id={"vir": to}, device_id_type=MESH)

    def two_copy(d):
        return pltpu.make_async_remote_copy(
            src_ref=picked.at[d if by_tile else 0],
            dst_ref=weights.at[:, :, pl.ds(pl.multiple_of(vir * piece, piece), piece), :],
            send_sem=two_send.at[d], recv_sem=two_recv.at[d],
            device_id={"vir": lax.rem(vir + d, n_vir)}, device_id_type=MESH)

    def own_rows():
        return pltpu.make_async_copy(
            picked.at[0], weights.at[:, :, pl.ds(pl.multiple_of(vir * piece, piece), piece), :], local_sem)

    def amp_copy(d):
        return pltpu.make_async_remote_copy(
            src_ref=amp_ref, dst_ref=amp_all.at[occ], send_sem=amp_send.at[d], recv_sem=amp_recv.at[d],
            device_id={"occ": lax.rem(occ + d, n_occ)}, device_id_type=MESH)

    def wait_one_from_stage(d):
        pltpu.make_async_remote_copy(
            src_ref=stage.at[0], dst_ref=got.at[vir], send_sem=one_send.at[d], recv_sem=one_recv.at[d],
            device_id={"vir": lax.rem(vir + d, n_vir)}, device_id_type=MESH).wait_recv()

    if by_tile:
        for d in range(1, n_vir):
            guarded(full, lax.rem(vir + d, n_vir) < relays, lambda d=d: info_copy(d).start())
    for d in range(1, n_vir):
        guarded(full, lax.rem(vir + d, n_vir) < relays, lambda d=d: one_copy(d).start())
    for d in range(1, n_occ):
        amp_copy(d).start()

    def relay():
        got[vir] = stage[vir]
        if by_tile:
            for d in range(1, n_vir):
                info_copy(d).wait_recv()
            to_smem = pltpu.make_async_copy(info_all, info_smem, local_sem)
            to_smem.start()
            to_smem.wait()
        for d in range(1, n_vir):
            wait_one_from_stage(d)
        owners = [owner_ref[s] for s in range(steps)]
        for d in list(range(1, n_vir)) + [0]:
            to = lax.rem(vir + d, n_vir)
            if by_tile:
                for t in range(tiles):
                    irrep = info_smem[to, 0, t]
                    for s in range(steps):
                        picked[d, t, s] = got[owners[s], irrep]
            elif d == 1 or n_vir == 1:
                for g in range(irreps):
                    for s in range(steps):
                        picked[0, g, s] = got[owners[s], g]
            if d:
                two_copy(d).start()
        own_rows().start()

    guarded(full, is_relay, relay)

    for d in range(1, n_occ):
        amp_copy(d).wait_recv()
    for d in range(1, n_vir):
        guarded(full, lax.rem(vir + n_vir - d, n_vir) < relays, lambda d=d: two_copy(d).wait_recv())

    fetches[4].wait()
    guarded(full, is_relay, lambda: own_rows().wait())
    for d in range(1, n_occ):
        amp_copy(d).wait_send()
    for d in range(1, n_vir):
        if by_tile:
            guarded(full, lax.rem(vir + d, n_vir) < relays, lambda d=d: info_copy(d).wait_send())
        guarded(full, lax.rem(vir + d, n_vir) < relays, lambda d=d: one_copy(d).wait_send())
        guarded(full, is_relay, lambda d=d: two_copy(d).wait_send())


def per_device(n_vir, n_occ, amplitudes, pair_irrep, integrals, panel_blocks, panel_owner):
    pair_dev, width = amplitudes.shape
    _, irreps, depth, columns = integrals.shape
    tiles = pair_irrep.shape[0]
    steps = panel_owner.shape[0]
    relays = min(n_vir, depth // ROWS)
    piece = depth // relays
    by_tile = tiles < irreps
    choices = min(tiles, irreps)
    lanes = -(-tiles // 128) * 128
    kind = amplitudes.dtype
    hbm = pl.BlockSpec(memory_space=pltpu.HBM)
    dma = pltpu.SemaphoreType.DMA
    gathered, weights = pl.pallas_call(
        functools.partial(ladder_kernel, n_vir, n_occ, relays, by_tile),
        out_shape=(
            pltpu.VMEM((tiles, pair_dev, width), kind),
            pltpu.VMEM((choices, steps, depth, columns), kind),
        ),
        in_specs=[hbm] * 5,
        out_specs=(pl.BlockSpec(memory_space=pltpu.VMEM),) * 2,
        scratch_shapes=[
            pltpu.SMEM(pair_irrep.shape, jnp.int32),
            pltpu.SMEM(panel_blocks.shape, jnp.int32),
            pltpu.SMEM(panel_owner.shape, jnp.int32),
            pltpu.VMEM(integrals.shape[1:], kind),
            pltpu.VMEM((1, lanes), jnp.int32),
            pltpu.VMEM((n_vir, 1, lanes), jnp.int32),
            pltpu.SMEM((n_vir, 1, lanes), jnp.int32),
            pltpu.VMEM((relays, irreps, piece, columns), kind),
            pltpu.VMEM((n_vir, irreps, piece, columns), kind),
            pltpu.VMEM((n_vir if by_tile else 1, choices, steps, piece, columns), kind),
            dma((n_vir,)), dma((n_vir,)), dma((n_vir,)), dma((n_vir,)),
            dma((n_vir,)), dma((n_vir,)), dma((n_occ,)), dma((n_occ,)), dma, dma((5,)),
        ],
        compiler_params=pltpu.CompilerParams(
            collective_id=0, has_side_effects=True, vmem_limit_bytes=60 * 1024 * 1024),
    )(pair_irrep, panel_blocks, panel_owner, amplitudes, integrals)
    weights = weights.reshape(choices, steps * depth, columns)
    if by_tile:
        result = jnp.einsum("tpk,tkc->tpc", gathered, weights, preferred_element_type=jnp.float32)
        return result.astype(kind).reshape(tiles * pair_dev, columns)

    def tile_ladder(inputs):
        rows, irrep = inputs
        chosen = lax.dynamic_index_in_dim(weights, irrep, 0, keepdims=False)
        return jnp.dot(rows, chosen, preferred_element_type=jnp.float32).astype(kind)

    return lax.map(tile_ladder, (gathered, pair_irrep)).reshape(tiles * pair_dev, columns)


def solution(mesh):
    return jax.shard_map(
        functools.partial(per_device, mesh.shape["vir"], mesh.shape["occ"]),
        mesh=mesh,
        in_specs=(
            P(("vir", "occ"), None),
            P("vir"),
            P("vir", None, None, "occ"),
            P("vir", None),
            P(),
        ),
        out_specs=P("vir", "occ"),
        check_vma=False,
    )
```

```python
import functools

import jax
import jax.numpy as jnp
from jax import lax
from jax.experimental import pallas as pl
from jax.experimental.pallas import tpu as pltpu
from jax.sharding import PartitionSpec as P

MESH = pl.DeviceIdType.MESH
ROWS = 16


def guarded(always, condition, run):
    if always:
        run()
    else:
        pl.when(condition)(run)


def ladder_kernel(
    n_vir, n_occ, relays, by_tile,
    labels_hbm, blocks_hbm, owner_hbm, amp_ref, panel_hbm, amp_all, weights,
    labels_ref, blocks_ref, owner_ref, panel_ref,
    info, info_all, info_smem, stage, got, picked,
    info_send, info_recv, one_send, one_recv, two_send, two_recv, amp_send, amp_recv, local_sem, fetch_sem,
):
    vir, occ = lax.axis_index("vir"), lax.axis_index("occ")
    irreps = panel_ref.shape[0]
    steps = owner_ref.shape[0]
    tiles = labels_ref.shape[0]
    piece = stage.shape[2]
    full = relays == n_vir
    is_relay = vir < relays
    both_ways = [d for near in range(1, n_vir // 2 + 1) for d in sorted({near, n_vir - near})]

    barrier = pltpu.get_barrier_semaphore()
    for d in range(1, n_vir):
        pl.semaphore_signal(barrier, inc=1, device_id={"vir": lax.rem(vir + d, n_vir)}, device_id_type=MESH)
    for d in range(1, n_occ):
        pl.semaphore_signal(barrier, inc=1, device_id={"occ": lax.rem(occ + d, n_occ)}, device_id_type=MESH)

    fetches = [
        pltpu.make_async_copy(labels_hbm, labels_ref, fetch_sem.at[0]),
        pltpu.make_async_copy(blocks_hbm, blocks_ref, fetch_sem.at[1]),
        pltpu.make_async_copy(owner_hbm, owner_ref, fetch_sem.at[2]),
        pltpu.make_async_copy(panel_hbm.at[0], panel_ref, fetch_sem.at[3]),
        pltpu.make_async_copy(amp_ref, amp_all.at[occ], fetch_sem.at[4]),
    ]
    for fetch in fetches:
        fetch.start()
    for fetch in fetches[:4]:
        fetch.wait()

    lanes = lax.broadcasted_iota(jnp.int32, info.shape, 1)
    row = jnp.zeros(info.shape, jnp.int32)
    for t in range(tiles):
        row = jnp.where(lanes == t, labels_ref[t], row)
    info[...] = row
    info_all[vir] = row
    for g in range(irreps):
        slot = jnp.int32(0)
        for b in range(irreps):
            slot = jnp.where(blocks_ref[0, b] == g, b, slot)
        block = panel_ref[slot]
        for w in range(relays):
            stage[w, g] = block[w * piece:(w + 1) * piece]

    pl.semaphore_wait(barrier, n_vir - 1 + n_occ - 1)

    def info_copy(d):
        return pltpu.make_async_remote_copy(
            src_ref=info, dst_ref=info_all.at[vir], send_sem=info_send.at[d], recv_sem=info_recv.at[d],
            device_id={"vir": lax.rem(vir + d, n_vir)}, device_id_type=MESH)

    def one_copy(d):
        to = lax.rem(vir + d, n_vir)
        return pltpu.make_async_remote_copy(
            src_ref=stage.at[to], dst_ref=got.at[vir], send_sem=one_send.at[d], recv_sem=one_recv.at[d],
            device_id={"vir": to}, device_id_type=MESH)

    def two_copy(d):
        return pltpu.make_async_remote_copy(
            src_ref=picked.at[d if by_tile else 0],
            dst_ref=weights.at[:, :, pl.ds(pl.multiple_of(vir * piece, piece), piece), :],
            send_sem=two_send.at[d], recv_sem=two_recv.at[d],
            device_id={"vir": lax.rem(vir + d, n_vir)}, device_id_type=MESH)

    def own_rows():
        return pltpu.make_async_copy(
            picked.at[0], weights.at[:, :, pl.ds(pl.multiple_of(vir * piece, piece), piece), :], local_sem)

    def amp_copy(d):
        return pltpu.make_async_remote_copy(
            src_ref=amp_ref, dst_ref=amp_all.at[occ], send_sem=amp_send.at[d], recv_sem=amp_recv.at[d],
            device_id={"occ": lax.rem(occ + d, n_occ)}, device_id_type=MESH)

    def wait_one_from_stage(d):
        pltpu.make_async_remote_copy(
            src_ref=stage.at[0], dst_ref=got.at[vir], send_sem=one_send.at[d], recv_sem=one_recv.at[d],
            device_id={"vir": lax.rem(vir + d, n_vir)}, device_id_type=MESH).wait_recv()

    if by_tile:
        for d in range(1, n_vir):
            guarded(full, lax.rem(vir + d, n_vir) < relays, lambda d=d: info_copy(d).start())
    for d in both_ways:
        guarded(full, lax.rem(vir + d, n_vir) < relays, lambda d=d: one_copy(d).start())
    def relay():
        got[vir] = stage[vir]
        if by_tile:
            for d in range(1, n_vir):
                info_copy(d).wait_recv()
            to_smem = pltpu.make_async_copy(info_all, info_smem, local_sem)
            to_smem.start()
            to_smem.wait()
        for d in range(1, n_vir):
            wait_one_from_stage(d)
        owners = [owner_ref[s] for s in range(steps)]
        for d in both_ways + [0]:
            to = lax.rem(vir + d, n_vir)
            if by_tile:
                for t in range(tiles):
                    irrep = info_smem[to, 0, t]
                    for s in range(steps):
                        picked[d, t, s] = got[owners[s], irrep]
            elif d == 1 or n_vir == 1:
                for g in range(irreps):
                    for s in range(steps):
                        picked[0, g, s] = got[owners[s], g]
            if d:
                two_copy(d).start()
        own_rows().start()

    guarded(full, is_relay, relay)
    for d in range(1, n_occ):
        amp_copy(d).start()

    for d in range(1, n_occ):
        amp_copy(d).wait_recv()
    for d in range(1, n_vir):
        guarded(full, lax.rem(vir + n_vir - d, n_vir) < relays, lambda d=d: two_copy(d).wait_recv())

    fetches[4].wait()
    guarded(full, is_relay, lambda: own_rows().wait())
    for d in range(1, n_occ):
        amp_copy(d).wait_send()
    for d in range(1, n_vir):
        if by_tile:
            guarded(full, lax.rem(vir + d, n_vir) < relays, lambda d=d: info_copy(d).wait_send())
        guarded(full, lax.rem(vir + d, n_vir) < relays, lambda d=d: one_copy(d).wait_send())
        guarded(full, is_relay, lambda d=d: two_copy(d).wait_send())


def per_device(n_vir, n_occ, amplitudes, pair_irrep, integrals, panel_blocks, panel_owner):
    pair_dev, width = amplitudes.shape
    _, irreps, depth, columns = integrals.shape
    tiles = pair_irrep.shape[0]
    steps = panel_owner.shape[0]
    relays = min(n_vir, depth // ROWS)
    piece = depth // relays
    by_tile = tiles < irreps
    choices = min(tiles, irreps)
    lanes = -(-tiles // 128) * 128
    kind = amplitudes.dtype
    hbm = pl.BlockSpec(memory_space=pltpu.HBM)
    dma = pltpu.SemaphoreType.DMA
    gathered, weights = pl.pallas_call(
        functools.partial(ladder_kernel, n_vir, n_occ, relays, by_tile),
        out_shape=(
            pltpu.VMEM((tiles, pair_dev, width), kind),
            pltpu.VMEM((choices, steps, depth, columns), kind),
        ),
        in_specs=[hbm] * 5,
        out_specs=(pl.BlockSpec(memory_space=pltpu.VMEM),) * 2,
        scratch_shapes=[
            pltpu.SMEM(pair_irrep.shape, jnp.int32),
            pltpu.SMEM(panel_blocks.shape, jnp.int32),
            pltpu.SMEM(panel_owner.shape, jnp.int32),
            pltpu.VMEM(integrals.shape[1:], kind),
            pltpu.VMEM((1, lanes), jnp.int32),
            pltpu.VMEM((n_vir, 1, lanes), jnp.int32),
            pltpu.SMEM((n_vir, 1, lanes), jnp.int32),
            pltpu.VMEM((relays, irreps, piece, columns), kind),
            pltpu.VMEM((n_vir, irreps, piece, columns), kind),
            pltpu.VMEM((n_vir if by_tile else 1, choices, steps, piece, columns), kind),
            dma((n_vir,)), dma((n_vir,)), dma((n_vir,)), dma((n_vir,)),
            dma((n_vir,)), dma((n_vir,)), dma((n_occ,)), dma((n_occ,)), dma, dma((5,)),
        ],
        compiler_params=pltpu.CompilerParams(
            collective_id=0, has_side_effects=True, vmem_limit_bytes=60 * 1024 * 1024),
    )(pair_irrep, panel_blocks, panel_owner, amplitudes, integrals)
    weights = weights.reshape(choices, steps * depth, columns)
    if by_tile:
        result = jnp.einsum("tpk,tkc->tpc", gathered, weights, preferred_element_type=jnp.float32)
        return result.astype(kind).reshape(tiles * pair_dev, columns)

    def tile_ladder(inputs):
        rows, irrep = inputs
        chosen = lax.dynamic_index_in_dim(weights, irrep, 0, keepdims=False)
        return jnp.dot(rows, chosen, preferred_element_type=jnp.float32).astype(kind)

    return lax.map(tile_ladder, (gathered, pair_irrep)).reshape(tiles * pair_dev, columns)


def solution(mesh):
    return jax.shard_map(
        functools.partial(per_device, mesh.shape["vir"], mesh.shape["occ"]),
        mesh=mesh,
        in_specs=(
            P(("vir", "occ"), None),
            P("vir"),
            P("vir", None, None, "occ"),
            P("vir", None),
            P(),
        ),
        out_specs=P("vir", "occ"),
        check_vma=False,
    )
```

```python
import functools

import jax
import jax.numpy as jnp
from jax import lax
from jax.experimental import pallas as pl
from jax.experimental.pallas import tpu as pltpu
from jax.sharding import PartitionSpec as P

MESH = pl.DeviceIdType.MESH
ROWS = 16


def guarded(always, condition, run):
    if always:
        run()
    else:
        pl.when(condition)(run)


def ladder_kernel(
    n_vir, n_occ, relays, by_tile,
    labels_hbm, blocks_hbm, owner_hbm, amp_ref, panel_hbm, amp_all, weights,
    labels_ref, blocks_ref, owner_ref, panel_ref,
    info, info_all, info_smem, stage, got, picked,
    info_send, info_recv, one_send, one_recv, two_send, two_recv, amp_send, amp_recv, local_sem, fetch_sem,
):
    vir, occ = lax.axis_index("vir"), lax.axis_index("occ")
    irreps = panel_ref.shape[0]
    steps = owner_ref.shape[0]
    tiles = labels_ref.shape[0]
    piece = stage.shape[2]
    full = relays == n_vir
    is_relay = vir < relays
    both_ways = [d for near in range(1, n_vir // 2 + 1) for d in sorted({near, n_vir - near})]

    barrier = pltpu.get_barrier_semaphore()
    for d in range(1, n_vir):
        pl.semaphore_signal(barrier, inc=1, device_id={"vir": lax.rem(vir + d, n_vir)}, device_id_type=MESH)
    for d in range(1, n_occ):
        pl.semaphore_signal(barrier, inc=1, device_id={"occ": lax.rem(occ + d, n_occ)}, device_id_type=MESH)

    fetches = [
        pltpu.make_async_copy(labels_hbm, labels_ref, fetch_sem.at[0]),
        pltpu.make_async_copy(blocks_hbm, blocks_ref, fetch_sem.at[1]),
        pltpu.make_async_copy(owner_hbm, owner_ref, fetch_sem.at[2]),
        pltpu.make_async_copy(panel_hbm.at[0], panel_ref, fetch_sem.at[3]),
        pltpu.make_async_copy(amp_ref, amp_all.at[occ], fetch_sem.at[4]),
    ]
    for fetch in fetches:
        fetch.start()
    for fetch in fetches[:4]:
        fetch.wait()

    lanes = lax.broadcasted_iota(jnp.int32, info.shape, 1)
    row = jnp.zeros(info.shape, jnp.int32)
    for t in range(tiles):
        row = jnp.where(lanes == t, labels_ref[t], row)
    info[...] = row
    info_all[vir] = row
    for g in range(irreps):
        slot = jnp.int32(0)
        for b in range(irreps):
            slot = jnp.where(blocks_ref[0, b] == g, b, slot)
        block = panel_ref[slot]
        for w in range(relays):
            stage[w, g] = block[w * piece:(w + 1) * piece]

    pl.semaphore_wait(barrier, n_vir - 1 + n_occ - 1)

    def info_copy(d):
        return pltpu.make_async_remote_copy(
            src_ref=info, dst_ref=info_all.at[vir], send_sem=info_send.at[0 if full else d], recv_sem=info_recv.at[0 if full else d],
            device_id={"vir": lax.rem(vir + d, n_vir)}, device_id_type=MESH)

    def one_copy(d):
        to = lax.rem(vir + d, n_vir)
        return pltpu.make_async_remote_copy(
            src_ref=stage.at[to], dst_ref=got.at[vir], send_sem=one_send.at[0 if full else d], recv_sem=one_recv.at[0 if full else d],
            device_id={"vir": to}, device_id_type=MESH)

    def two_copy(d):
        return pltpu.make_async_remote_copy(
            src_ref=picked.at[d if by_tile else 0],
            dst_ref=weights.at[:, :, pl.ds(pl.multiple_of(vir * piece, piece), piece), :],
            send_sem=two_send.at[0 if full else d], recv_sem=two_recv.at[0 if full else d],
            device_id={"vir": lax.rem(vir + d, n_vir)}, device_id_type=MESH)

    def own_rows():
        return pltpu.make_async_copy(
            picked.at[0], weights.at[:, :, pl.ds(pl.multiple_of(vir * piece, piece), piece), :], local_sem)

    def amp_copy(d):
        return pltpu.make_async_remote_copy(
            src_ref=amp_ref, dst_ref=amp_all.at[occ], send_sem=amp_send.at[d], recv_sem=amp_recv.at[d],
            device_id={"occ": lax.rem(occ + d, n_occ)}, device_id_type=MESH)

    def wait_one_from_stage(d):
        pltpu.make_async_remote_copy(
            src_ref=stage.at[0], dst_ref=got.at[vir], send_sem=one_send.at[0 if full else d], recv_sem=one_recv.at[0 if full else d],
            device_id={"vir": lax.rem(vir + d, n_vir)}, device_id_type=MESH).wait_recv()

    def wait_all(semaphore, like):
        pltpu.make_async_copy(like, like, semaphore.at[0]).wait()

    others = n_vir - 1
    all_info = info_all.at[pl.ds(0, others)]
    all_one = got.at[pl.ds(0, others)]
    all_two = weights.at[:, :, pl.ds(0, others * piece), :] if full else None

    if by_tile:
        for d in range(1, n_vir):
            guarded(full, lax.rem(vir + d, n_vir) < relays, lambda d=d: info_copy(d).start())
    for d in both_ways:
        guarded(full, lax.rem(vir + d, n_vir) < relays, lambda d=d: one_copy(d).start())
    def relay():
        got[vir] = stage[vir]
        if by_tile:
            if full:
                wait_all(info_recv, all_info)
            for d in range(1, 1 if full else n_vir):
                info_copy(d).wait_recv()
            to_smem = pltpu.make_async_copy(info_all, info_smem, local_sem)
            to_smem.start()
            to_smem.wait()
        if full:
            wait_all(one_recv, all_one)
        for d in range(1, 1 if full else n_vir):
            wait_one_from_stage(d)
        owners = [owner_ref[s] for s in range(steps)]
        for d in both_ways + [0]:
            to = lax.rem(vir + d, n_vir)
            if by_tile:
                for t in range(tiles):
                    irrep = info_smem[to, 0, t]
                    for s in range(steps):
                        picked[d, t, s] = got[owners[s], irrep]
            elif d == 1 or n_vir == 1:
                for g in range(irreps):
                    for s in range(steps):
                        picked[0, g, s] = got[owners[s], g]
            if d:
                two_copy(d).start()
        own_rows().start()

    guarded(full, is_relay, relay)
    for d in range(1, n_occ):
        amp_copy(d).start()

    for d in range(1, n_occ):
        amp_copy(d).wait_recv()
    if full:
        wait_all(two_recv, all_two)
    for d in range(1, 1 if full else n_vir):
        guarded(full, lax.rem(vir + n_vir - d, n_vir) < relays, lambda d=d: two_copy(d).wait_recv())

    fetches[4].wait()
    guarded(full, is_relay, lambda: own_rows().wait())
    for d in range(1, n_occ):
        amp_copy(d).wait_send()
    if full:
        if by_tile:
            wait_all(info_send, all_info)
        wait_all(one_send, all_one)
        wait_all(two_send, all_two)
    for d in range(1, 1 if full else n_vir):
        if by_tile:
            guarded(full, lax.rem(vir + d, n_vir) < relays, lambda d=d: info_copy(d).wait_send())
        guarded(full, lax.rem(vir + d, n_vir) < relays, lambda d=d: one_copy(d).wait_send())
        guarded(full, is_relay, lambda d=d: two_copy(d).wait_send())


def per_device(n_vir, n_occ, amplitudes, pair_irrep, integrals, panel_blocks, panel_owner):
    pair_dev, width = amplitudes.shape
    _, irreps, depth, columns = integrals.shape
    tiles = pair_irrep.shape[0]
    steps = panel_owner.shape[0]
    relays = min(n_vir, depth // ROWS)
    piece = depth // relays
    by_tile = tiles < irreps
    choices = min(tiles, irreps)
    lanes = -(-tiles // 128) * 128
    kind = amplitudes.dtype
    hbm = pl.BlockSpec(memory_space=pltpu.HBM)
    dma = pltpu.SemaphoreType.DMA
    gathered, weights = pl.pallas_call(
        functools.partial(ladder_kernel, n_vir, n_occ, relays, by_tile),
        out_shape=(
            pltpu.VMEM((tiles, pair_dev, width), kind),
            pltpu.VMEM((choices, steps, depth, columns), kind),
        ),
        in_specs=[hbm] * 5,
        out_specs=(pl.BlockSpec(memory_space=pltpu.VMEM),) * 2,
        scratch_shapes=[
            pltpu.SMEM(pair_irrep.shape, jnp.int32),
            pltpu.SMEM(panel_blocks.shape, jnp.int32),
            pltpu.SMEM(panel_owner.shape, jnp.int32),
            pltpu.VMEM(integrals.shape[1:], kind),
            pltpu.VMEM((1, lanes), jnp.int32),
            pltpu.VMEM((n_vir, 1, lanes), jnp.int32),
            pltpu.SMEM((n_vir, 1, lanes), jnp.int32),
            pltpu.VMEM((relays, irreps, piece, columns), kind),
            pltpu.VMEM((n_vir, irreps, piece, columns), kind),
            pltpu.VMEM((n_vir if by_tile else 1, choices, steps, piece, columns), kind),
            dma((n_vir,)), dma((n_vir,)), dma((n_vir,)), dma((n_vir,)),
            dma((n_vir,)), dma((n_vir,)), dma((n_occ,)), dma((n_occ,)), dma, dma((5,)),
        ],
        compiler_params=pltpu.CompilerParams(
            collective_id=0, has_side_effects=True, vmem_limit_bytes=60 * 1024 * 1024),
    )(pair_irrep, panel_blocks, panel_owner, amplitudes, integrals)
    weights = weights.reshape(choices, steps * depth, columns)
    if by_tile:
        result = jnp.einsum("tpk,tkc->tpc", gathered, weights, preferred_element_type=jnp.float32)
        return result.astype(kind).reshape(tiles * pair_dev, columns)

    def tile_ladder(inputs):
        rows, irrep = inputs
        chosen = lax.dynamic_index_in_dim(weights, irrep, 0, keepdims=False)
        return jnp.dot(rows, chosen, preferred_element_type=jnp.float32).astype(kind)

    return lax.map(tile_ladder, (gathered, pair_irrep)).reshape(tiles * pair_dev, columns)


def solution(mesh):
    return jax.shard_map(
        functools.partial(per_device, mesh.shape["vir"], mesh.shape["occ"]),
        mesh=mesh,
        in_specs=(
            P(("vir", "occ"), None),
            P("vir"),
            P("vir", None, None, "occ"),
            P("vir", None),
            P(),
        ),
        out_specs=P("vir", "occ"),
        check_vma=False,
    )
```
